256 devices in a mesh: depth: 16 (over z, core), row: 4 (over x), col: 4 (over y).
Axes of the slice: x: 4, y: 4, z: 8, core: 2. Of those that a mesh axis runs over, the one named last changes fastest.
Arguments:
- tile_left: bfloat16 [16, 16, 64, 1024], P('row', 'col'), may hold values from -6 to 6
- tile_right: bfloat16 [16, 16, 64, 1024], P('row', 'col'), may hold values from -6 to 6
- row_left: bfloat16 [16, 64, 64, 1024], P('row', 'depth', None, 'col'), may hold values from -6 to 6
- row_right: bfloat16 [16, 64, 64, 1024], P('row', 'depth', None, 'col'), may hold values from -0.1875 to 0.1875
- col_left: bfloat16 [16, 64, 64, 1024], P('col', 'depth', None, 'row'), may hold values from -6 to 6
- col_right: bfloat16 [16, 64, 64, 1024], P('col', 'depth', None, 'row'), may hold values from -0.1875 to 0.1875
- row_mask: int32 [16, 64], P('row', 'depth'), may hold values 0 or 1
- col_mask: int32 [16, 64], P('col', 'depth'), may hold values 0 or 1
- sketch: bfloat16 [64, 1024], replicated, may hold values from -1 to 1
Outputs:
- new_left: float32 [16, 16, 64, 1024], P('row', 'col', 'depth')
- new_right: float32 [16, 16, 64, 1024], P('row', 'col', 'depth')
The draws below stay inside these ranges and needn't reach their ends.
All inputs are finite; a program needn't handle non-finite values. No bound on the sum of `row_mask` or of `col_mask` on one device may be relied on, other than what follows from the above.
Results may differ from the reference program's by a relative error of at most 0.0003.
Values may be sent and summed in bfloat16 or wider, within the bound.
A program may use at most 64 MiB of HBM per device.

```python
import math
import jax
import jax.numpy as jnp
from jax import lax

NB = 1024
K = 64
TR = 16
TC = 16
PANEL = 64


def draw_sketch(key, part):
    key_rows = jax.random.fold_in(key, 11)
    key_gains = jax.random.fold_in(key, 12)
    entries = jnp.clip(jax.random.normal(key_rows, (K, NB), jnp.float32), -5.0, 5.0)
    gains = jax.random.uniform(key_gains, (K, 1), jnp.float32, 0.75, 1.25)
    entries = gains * entries / math.sqrt(NB)
    return jnp.clip(entries, -1.0, 1.0).astype(jnp.bfloat16)


def factor_entries(key, shape):
    key_vals = jax.random.fold_in(key, 21)
    entries = jnp.clip(jax.random.normal(key_vals, shape, jnp.float32), -6.0, 6.0)
    return entries.astype(jnp.bfloat16)


def draw_tile_left(key, part):
    return factor_entries(jax.random.fold_in(key, 31), (TR, TC, K, NB))


def draw_tile_right(key, part):
    return factor_entries(jax.random.fold_in(key, 32), (TR, TC, K, NB))


def draw_row_left(key, part):
    return factor_entries(jax.random.fold_in(key, 33), (TR, PANEL, K, NB))


def draw_col_left(key, part):
    return factor_entries(jax.random.fold_in(key, 34), (TC, PANEL, K, NB))


def touch_ends(values, key, least, largest):
    longest = values.shape.index(max(values.shape))
    spots = []
    for shift in (0, 1):
        where = [jax.random.randint(jax.random.fold_in(key, axis), (), 0, length) for axis, length in enumerate(values.shape)]
        where[longest] = (where[longest] + shift) % values.shape[longest]
        spots.append(tuple(where))
    return values.at[spots[0]].set(least).at[spots[1]].set(largest)


def levels(stream_key, dims, pieces, least, high):
    factor_of = 1.0
    for position, blocks in pieces:
        steps = jax.random.uniform(jax.random.fold_in(jax.random.fold_in(stream_key, 6), position), (blocks,), jnp.float32, least / len(pieces), high / len(pieces))
        factor_of = factor_of * jnp.repeat(jnp.exp(steps), dims[position] // blocks).reshape((-1,) + (1,) * (len(dims) - 1 - position))
    return factor_of


def scatter_about(stream_key, dims, width, limit, shards=(), dtype=jnp.bfloat16):
    result = width * jax.random.normal(stream_key, dims, jnp.float32)
    if shards:
        result = result * levels(stream_key, dims, shards, -0.22, 0.18)
    return jnp.clip(result, -limit, limit).astype(dtype)


def setup_inputs(seed: int = 0) -> dict:
    streams_of = jax.random.split(jax.random.key(seed), 10)
    return {
        "tile_left": draw_tile_left(jax.random.fold_in(streams_of[9], 71), 0),
        "tile_right": draw_tile_right(jax.random.fold_in(streams_of[9], 71), 0),
        "row_left": draw_row_left(jax.random.fold_in(streams_of[9], 71), 0),
        "row_right": scatter_about(streams_of[3], (TR, PANEL, K, NB), NB ** -0.5, 0.1875, ((0, 4), (1, 16), (3, 4))),
        "col_left": draw_col_left(jax.random.fold_in(streams_of[9], 71), 0),
        "col_right": scatter_about(streams_of[5], (TC, PANEL, K, NB), NB ** -0.5, 0.1875, ((0, 4), (1, 16), (3, 4))),
        "row_mask": touch_ends((jax.random.randint(streams_of[6], (TR, PANEL), 0, 4) < 3).astype(jnp.int32), jax.random.fold_in(streams_of[6], 1), 0, 1),
        "col_mask": touch_ends((jax.random.randint(streams_of[7], (TC, PANEL), 0, 4) < 3).astype(jnp.int32), jax.random.fold_in(streams_of[7], 1), 0, 1),
        "sketch": draw_sketch(jax.random.fold_in(streams_of[9], 71), 0),
    }


exact_mode = lax.Precision.HIGHEST

def orthonormalize(sketched):
    for repeat in range(2):
        gram_mat = jnp.einsum('jtn,jsn->jts', sketched, sketched, precision=exact_mode)
        factor = jnp.linalg.cholesky(gram_mat)
        sketched = jax.scipy.linalg.solve_triangular(factor, sketched, lower=True)
    return sketched

def reference(tile_left, tile_right, row_left, row_right, col_left, col_right, row_mask, col_mask, sketch):
    sketch_full = sketch.astype(jnp.float32)
    col_left_full = col_left.astype(jnp.float32)
    col_right_full = col_right.astype(jnp.float32)
    col_sketch = jnp.einsum('jksn,tn->jkst', col_left_full, sketch_full, precision=exact_mode)
    col_weight = col_mask.astype(jnp.float32)

    def one_row(items):
        left_row, right_row, mask_row, tile_l, tile_r = items
        left_row = left_row.astype(jnp.float32)
        tile_l = tile_l.astype(jnp.float32)
        tile_r = tile_r.astype(jnp.float32)
        coupling = jnp.einsum('krn,jksn->jkrs', right_row.astype(jnp.float32), col_right_full, precision=exact_mode)
        coupling = coupling * (mask_row.astype(jnp.float32)[None, :] * col_weight)[:, :, None, None]
        mixing = jnp.einsum('jkrs,jkst->jkrt', coupling, col_sketch, precision=exact_mode)
        sketch_right = jnp.einsum('jrn,tn->jrt', tile_r, sketch_full, precision=exact_mode)
        sketched = jnp.einsum('jrt,jrn->jtn', sketch_right, tile_l, precision=exact_mode)
        sketched = sketched - jnp.einsum('jkrt,krn->jtn', mixing, left_row, precision=exact_mode)
        basis = orthonormalize(sketched)
        basis_row = jnp.einsum('jtn,krn->jktr', basis, left_row, precision=exact_mode)
        projected = jnp.einsum('jktr,jkrs->jkts', basis_row, coupling, precision=exact_mode)
        own_part = jnp.einsum('jtn,jrn->jtr', basis, tile_l, precision=exact_mode)
        right_new = jnp.einsum('jtr,jrn->jtn', own_part, tile_r, precision=exact_mode)
        right_new = right_new - jnp.einsum('jkts,jksn->jtn', projected, col_left_full, precision=exact_mode)
        return (basis * math.sqrt(NB), right_new / math.sqrt(NB))
    new_left, new_right = lax.map(one_row, (row_left, row_right, row_mask, tile_left, tile_right))
    return (new_left, new_right)
```

```python
import math

import jax
import jax.numpy as jnp
from jax import lax
from jax.experimental import pallas as pl
from jax.experimental.pallas import tpu as pltpu
from jax.sharding import PartitionSpec as P

NB = 1024
K = 64
MESH = pl.DeviceIdType.MESH
F32 = jnp.float32
BF16 = jnp.bfloat16
HI = lax.Precision.HIGHEST
NZ = 8
NX = 4
CH = NB // NX


def dot_nn(a, b):
    return lax.dot_general(a, b, (((1,), (0,)), ((), ())), preferred_element_type=F32)


def dot_nt(a, b):
    return lax.dot_general(a, b, (((1,), (1,)), ((), ())), preferred_element_type=F32)


def split2(v):
    hi = v.astype(BF16)
    lo = (v - hi.astype(F32)).astype(BF16)
    return hi, lo


def split3(v):
    hi = v.astype(BF16)
    rest = v - hi.astype(F32)
    mid = rest.astype(BF16)
    lo = (rest - mid.astype(F32)).astype(BF16)
    return hi, mid, lo


def kernel(
    rm, cm, tl_in, tr_in, rl_in, rr_in, cl_in, cr_in, sk,
    outl, outr,
    RR, RL, CR, CL, SWR, BDh, BDl, CS, MX, S, SG, RT, RSP, RSM, RQP, RQM,
    TT, TLO, TRO, X, Q, WW, BC, FSL, FSR, FRL, FRR,
    ssem, rsem, lsem,
):
    d = lax.axis_index("depth")
    x = lax.axis_index("row")
    y = lax.axis_index("col")
    c = lax.rem(d, 2)
    o = 1 - c
    z = lax.div(d, 2)

    def zdev(k):
        return (lax.rem(z + k, NZ) * 2 + c, x, y)

    def xdev(k):
        return (d, lax.rem(x + k, NX), y)

    def ydev(k):
        return (d, x, lax.rem(y + k, NX))

    sib = (z * 2 + o, x, y)

    def chunk(base, k):
        return lax.rem(base + k, NX)

    names = {}
    descs = {}

    def send(name, src, dst, dev):
        n = names.setdefault(name, len(names))
        copy = pltpu.make_async_remote_copy(
            src_ref=src, dst_ref=dst, send_sem=ssem.at[n], recv_sem=rsem.at[n],
            device_id=dev, device_id_type=MESH,
        )
        copy.start()
        descs[name] = copy

    def recv(name):
        descs[name].wait_recv()

    barrier = pltpu.get_barrier_semaphore()
    partners = [zdev(k) for k in range(1, NZ)] + [xdev(1), xdev(3), ydev(1), ydev(3), sib]
    for dev in partners:
        pl.semaphore_signal(barrier, inc=1, device_id=dev, device_id_type=MESH)
    tile_i = 2 * c + lax.div(z, 4)
    tile_j = lax.rem(z, 4)
    local = [
        pltpu.make_async_copy(rl_in.at[pl.ds(2 * c, 2)], RL.at[y, :, pl.ds(4 * c, 4)], lsem.at[0]),
        pltpu.make_async_copy(cl_in, CL.at[x, :, pl.ds(4 * c, 4)], lsem.at[1]),
        pltpu.make_async_copy(tl_in.at[tile_i, tile_j], TLO, lsem.at[2]),
        pltpu.make_async_copy(tr_in.at[tile_i, tile_j], TRO, lsem.at[3]),
    ]
    for copy in local:
        copy.start()

    def masked(v, m):
        return (v.astype(F32) * m.astype(F32)).astype(BF16)

    def prep_row(n, _):
        ii, kk = lax.div(n, 4), lax.rem(n, 4)
        RR[y, ii, 4 * c + kk] = masked(rr_in[2 * c + ii, kk], rm[2 * c + ii, kk])
        SWR[ii, kk] = masked(rr_in[2 * o + ii, kk], rm[2 * o + ii, kk])
        return 0

    def prep_col(n, _):
        jj, kk = lax.div(n, 4), lax.rem(n, 4)
        CR[x, jj, 4 * c + kk] = masked(cr_in[jj, kk], cm[jj, kk])
        return 0

    lax.fori_loop(0, 8, prep_row, 0)
    lax.fori_loop(0, 16, prep_col, 0)
    pl.semaphore_wait(barrier, len(partners))

    def grp(buf, b, g):
        return buf.at[b, :, pl.ds(4 * g, 4)]

    def half(buf, a, h, g):
        return buf.at[a, pl.ds(2 * h, 2), pl.ds(4 * g, 4)]

    def row_own(t, buf, src, swap_src):
        send(t + "sw", swap_src, grp(buf, y, c), sib)
        send(t + "y+c", src, grp(buf, y, c), ydev(1))
        send(t + "y-c", src, grp(buf, y, c), ydev(3))

    def row_sib(t, buf):
        recv(t + "sw")
        send(t + "y+o", grp(buf, y, o), grp(buf, y, o), ydev(1))
        send(t + "y-o", grp(buf, y, o), grp(buf, y, o), ydev(3))

    def col_own(t, buf, src):
        send(t + "x+0", src.at[pl.ds(0, 2)], half(buf, x, 0, c), xdev(1))
        send(t + "x-1", src.at[pl.ds(2, 2)], half(buf, x, 1, c), xdev(3))
        send(t + "x+1", src.at[pl.ds(2, 2)], half(buf, x, 1, c), xdev(1))
        send(t + "x-0", src.at[pl.ds(0, 2)], half(buf, x, 0, c), xdev(3))
        send(t + "s", src, buf.at[x, :, pl.ds(4 * c, 4)], sib)

    def col_copy(t, came, buf, a, h):
        recv(t + came)
        send(t + "s" + came, half(buf, a, h, c), half(buf, a, h, c), sib)

    def forward_first(t, rbuf, cbuf):
        recv(t + "y+c")
        send(t + "y+f", grp(rbuf, chunk(y, 3), c), grp(rbuf, chunk(y, 3), c), ydev(1))
        col_copy(t, "x+0", cbuf, chunk(x, 3), 0)
        send(t + "x+f", half(cbuf, chunk(x, 3), 0, c), half(cbuf, chunk(x, 3), 0, c), xdev(1))
        col_copy(t, "x-1", cbuf, chunk(x, 1), 1)
        send(t + "x-f", half(cbuf, chunk(x, 1), 1, c), half(cbuf, chunk(x, 1), 1, c), xdev(3))

    def forward_second(t, rbuf, cbuf):
        recv(t + "y-o")
        send(t + "y-f", grp(rbuf, chunk(y, 1), o), grp(rbuf, chunk(y, 1), o), ydev(3))
        col_copy(t, "x+1", cbuf, chunk(x, 3), 1)
        col_copy(t, "x-0", cbuf, chunk(x, 1), 0)

    def gather_end(t, cbuf):
        col_copy(t, "x+f", cbuf, chunk(x, 2), 0)
        col_copy(t, "x-f", cbuf, chunk(x, 2), 1)
        for came in ("y+o", "y-c", "y+f", "y-f"):
            recv(t + came)
        for came in ("", "x+0", "x-1", "x+1", "x-0", "x+f", "x-f"):
            recv(t + "s" + came)

    row_own("R", RR, grp(RR, y, c), SWR)
    col_own("R", CR, CR.at[x, :, pl.ds(4 * c, 4)])
    row_sib("R", RR)
    send("Lsw", rl_in.at[pl.ds(2 * o, 2)], grp(RL, y, c), sib)
    forward_first("R", RR, CR)
    forward_second("R", RR, CR)
    send("Ly+c", rl_in.at[pl.ds(2 * c, 2)], grp(RL, y, c), ydev(1))
    send("Ly-c", rl_in.at[pl.ds(2 * c, 2)], grp(RL, y, c), ydev(3))
    col_own("L", CL, cl_in)
    row_sib("L", RL)

    for copy in local:
        copy.wait()
    h, m, l = split3(dot_nt(sk[...], TRO[...]))
    own = dot_nn(jnp.concatenate([h, m, l], axis=0), TLO[...])
    TT[...] = own[0:K] + own[K:2 * K] + own[2 * K:]

    gather_end("R", CR)

    blocks = lax.broadcasted_iota(jnp.int32, (256, 256), 0) // K == lax.broadcasted_iota(jnp.int32, (256, 256), 1) // K

    def couple(n, _):
        q, g = lax.div(n, 2), lax.rem(n, 2)
        i, j = lax.div(q, 4), lax.rem(q, 4)
        acc = jnp.zeros((256, 256), F32)
        for b in range(NX):
            acc = acc + dot_nt(
                RR[b, i, pl.ds(4 * g, 4)].reshape(256, CH), CR[b, j, pl.ds(4 * g, 4)].reshape(256, CH)
            )
        hi, lo = split2(jnp.where(blocks, -acc, 0.0))
        BDh[q, g] = hi
        BDl[q, g] = lo
        return 0

    lax.fori_loop(0, 16, couple, 0)

    forward_first("L", RL, CL)
    forward_second("L", RL, CL)
    gather_end("L", CL)

    def col_sketch(j, _):
        acc = jnp.zeros((K, 512), F32)
        for a in range(NX):
            acc = acc + dot_nt(sk[:, CH * a:CH * (a + 1)], CL[a, j].reshape(512, CH))
        hi, lo = split2(acc)
        CS[j, 0:K] = hi
        CS[j, K:2 * K] = lo
        return 0

    lax.fori_loop(0, 4, col_sketch, 0)

    def mix_tile(q, _):
        j = lax.rem(q, 4)
        for g in range(2):
            both = CS[j, :, 256 * g:256 * (g + 1)]
            p = dot_nt(both, BDh[q, g])
            mix = p[0:K] + p[K:] + dot_nt(both[0:K], BDl[q, g])
            hi, lo = split2(mix)
            MX[q, 0:K, 256 * g:256 * (g + 1)] = hi
            MX[q, K:2 * K, 256 * g:256 * (g + 1)] = lo
        return 0

    lax.fori_loop(0, 8, mix_tile, 0)

    def s_tile(q):
        i = lax.div(q, 4)
        both = MX[q]
        for b in range(NX):
            p = dot_nn(both, RL[b, i].reshape(512, CH))
            S[q, :, CH * b:CH * (b + 1)] = p[0:K] + p[K:]

    def up(s):
        return lax.rem(z + NZ - 1 - s, NZ)

    def down(s):
        return lax.rem(z + 1 + s, NZ)

    for s in range(NZ - 1):
        if s == 0:
            s_tile(up(0))
        for u in range(2):
            if s > 0:
                recv(f"S+{s - 1}{u}")
                S[up(s), 16 * u:16 * u + 16] += RSP[s - 1, u]
            send(f"S+{s}{u}", S.at[up(s), pl.ds(16 * u, 16)], RSP.at[s, u], zdev(1))
        if s == 0:
            s_tile(down(0))
        for u in range(2, 4):
            if s > 0:
                recv(f"S-{s - 1}{u}")
                S[down(s), 16 * u:16 * u + 16] += RSM[s - 1, u - 2]
            send(f"S-{s}{u}", S.at[down(s), pl.ds(16 * u, 16)], RSM.at[s, u - 2], zdev(NZ - 1))
        if s < 3:
            s_tile(up(s + 1))
        if s < 2:
            s_tile(down(s + 1))
        if s == 3:
            s_tile(z)
    for u in range(2):
        recv(f"S+{NZ - 2}{u}")
        rows = slice(16 * u, 16 * u + 16)
        SG[z, rows] = S[z, rows] + RSP[NZ - 2, u] + TT[rows]
    for u in range(2, 4):
        recv(f"S-{NZ - 2}{u}")
        rows = slice(16 * u, 16 * u + 16)
        SG[z, rows] = S[z, rows] + RSM[NZ - 2, u - 2] + TT[rows]

    def pass_on(s, way, hs):
        owner = lax.rem(z + NZ - (s - 1), NZ) if way == "+" else lax.rem(z + s - 1, NZ)
        for h in hs:
            if s > 1:
                recv(f"G{way}{s - 1}{h}")
            part = SG.at[owner, pl.ds(32 * h, 32)]
            send(f"G{way}{s}{h}", part, part, zdev(1 if way == "+" else NZ - 1))

    def tile_back(q):
        i = lax.div(q, 4)
        hi, lo = split2(SG[q])
        both = jnp.concatenate([hi, lo], axis=0)
        acc = jnp.zeros((2 * K, 512), F32)
        for b in range(NX):
            acc = acc + dot_nt(both[:, CH * b:CH * (b + 1)], RL[b, i].reshape(512, CH))
        hi, lo = split2(acc[0:K] + acc[K:])
        both = jnp.concatenate([hi, lo], axis=0)
        for g in range(2):
            cols = slice(256 * g, 256 * (g + 1))
            p = dot_nn(both[:, cols], BDh[q, g])
            BC[q, :, cols] = p[0:K] + p[K:] + dot_nn(hi[:, cols], BDl[q, g])

    lane = lax.broadcasted_iota(jnp.int32, (K, 2 * K), 1)
    sub = lax.broadcasted_iota(jnp.int32, (K, 2 * K), 0)
    lane1 = lax.broadcasted_iota(jnp.int32, (1, 2 * K), 1)
    sub1 = lax.broadcasted_iota(jnp.int32, (K, 1), 0)

    def inverse_factor(v):
        wide = jnp.concatenate([v, jnp.zeros_like(v)], axis=0)
        gram = lax.dot_general(v, wide, (((1,), (1,)), ((), ())), precision=HI, preferred_element_type=F32)
        X[...] = jnp.where(lane == sub + K, 1.0, gram)

        def step(n, _):
            full = X[...]
            row = X[pl.ds(n, 1), :]
            pivot = jnp.sum(jnp.where(lane1 == n, row, 0.0), axis=1, keepdims=True)
            col = jnp.sum(jnp.where(lane == n, full, 0.0), axis=1, keepdims=True)
            X[...] = full - jnp.where(sub1 > n, col, 0.0) * (row / pivot)
            return 0

        lax.fori_loop(0, K, step, 0)
        full = X[...]
        pivots = jnp.sum(jnp.where(lane == sub, full, 0.0), axis=1, keepdims=True)
        return full[:, K:] * (1.0 / jnp.sqrt(pivots))

    def dot_hi(a, b):
        return lax.dot_general(a, b, (((1,), (0,)), ((), ())), precision=HI, preferred_element_type=F32)

    pass_on(1, "+", (0, 1))
    pass_on(1, "-", (1, 0))
    first = inverse_factor(SG[z])
    WW[z] = first
    Q[...] = dot_hi(first, SG[z])
    pass_on(2, "+", (0, 1))
    pass_on(2, "-", (1, 0))
    tile_back(lax.rem(z + 7, NZ))
    tile_back(lax.rem(z + 1, NZ))
    second = inverse_factor(Q[...])
    WW[z] = dot_hi(second, WW[z])
    for k in range(1, NZ):
        send(f"W{k}", WW.at[z], WW.at[z], zdev(k))
    pass_on(3, "+", (0, 1))
    pass_on(3, "-", (1, 0))
    tile_back(lax.rem(z + 6, NZ))
    tile_back(lax.rem(z + 2, NZ))
    tile_back(z)
    pass_on(4, "+", (0,))
    pass_on(4, "-", (1,))
    h, m, l = split3(dot_hi(WW[z], SG[z]))
    own = dot_nt(jnp.concatenate([h, m, l], axis=0), TLO[...])
    h, m, l = split3(own[0:K] + own[K:2 * K] + own[2 * K:])
    own = dot_nn(jnp.concatenate([h, m, l], axis=0), TRO[...])
    TT[...] = own[0:K] + own[K:2 * K] + own[2 * K:]
    recv("G+31")
    tile_back(lax.rem(z + 5, NZ))
    recv("G-30")
    tile_back(lax.rem(z + 3, NZ))
    recv("G+40")
    recv("G-41")
    tile_back(lax.rem(z + 4, NZ))
    for k in range(1, NZ):
        recv(f"W{k}")

    def right_tile(q, _):
        j = lax.rem(q, 4)
        hi, lo = split2(dot_hi(WW[q], BC[q]))
        both = jnp.concatenate([hi, lo], axis=0)
        mine = jnp.where(q == z, 1.0, 0.0)
        for a in range(NX):
            cols = slice(CH * a, CH * (a + 1))
            p = dot_nn(both, CL[a, j].reshape(512, CH))
            RT[q, :, cols] = p[0:K] + p[K:] + mine * TT[:, cols]
        return 0

    def rows_of(chip):
        return pl.ds(pl.multiple_of(8 * chip, 8), 8)

    keep0 = c == 0
    scale = math.sqrt(NB)

    def basis_rows(q):
        v = scale * dot_hi(WW[q, rows_of(z), :], SG[q])
        FSL[4 * q:4 * q + 4] = jnp.where(keep0, v[4:8], v[0:4])
        outl[2 * c + q // 4, q % 4] = jnp.where(keep0, v[0:4], v[4:8])

    lax.fori_loop(0, 4, right_tile, 0)
    for s in range(NZ - 1):
        for u in range(2):
            tiles = slice(2 * u, 2 * u + 2)
            if s > 0:
                recv(f"P+{s - 1}{u}")
                RT[tiles, rows_of(up(s))] += RQP[s - 1, u]
            send(f"P+{s}{u}", RT.at[pl.ds(2 * u, 2), rows_of(up(s))], RQP.at[s, u], zdev(1))
        if s == 0:
            lax.fori_loop(4, 8, right_tile, 0)
        for u in range(2, 4):
            tiles = slice(2 * u, 2 * u + 2)
            if s > 0:
                recv(f"P-{s - 1}{u}")
                RT[tiles, rows_of(down(s))] += RQM[s - 1, u - 2]
            send(f"P-{s}{u}", RT.at[pl.ds(2 * u, 2), rows_of(down(s))], RQM.at[s, u - 2], zdev(NZ - 1))
        if s == 0:
            basis_rows(7)
        basis_rows(s)
    send("FL", FSL, FRL, sib)

    for u in range(4):
        way, buf = ("+", RQP) if u < 2 else ("-", RQM)
        recv(f"P{way}{NZ - 2}{u}")
        for q in (2 * u, 2 * u + 1):
            v = (1.0 / scale) * (RT[q, rows_of(z)] + buf[NZ - 2, u % 2, q % 2])
            FSR[4 * q:4 * q + 4] = jnp.where(keep0, v[4:8], v[0:4])
            outr[2 * c + q // 4, q % 4] = jnp.where(keep0, v[0:4], v[4:8])
    send("FR", FSR, FRR, sib)
    recv("FL")
    for q in range(8):
        outl[2 * o + q // 4, q % 4] = FRL[4 * q:4 * q + 4]
    recv("FR")
    for q in range(8):
        outr[2 * o + q // 4, q % 4] = FRR[4 * q:4 * q + 4]
    for copy in descs.values():
        copy.wait_send()


N_COPIES = 2 * (7 + 6 + 7) + 28 + 14 + 7 + 28 + 2


def on_device(
    tile_left, tile_right, row_left, row_right, col_left, col_right, row_mask, col_mask, sketch
):
    vmem = pl.BlockSpec(memory_space=pltpu.VMEM)
    smem = pl.BlockSpec(memory_space=pltpu.SMEM)
    hbm = pl.BlockSpec(memory_space=pl.ANY)
    out = jax.ShapeDtypeStruct((4, 4, 4, NB), F32)
    return pl.pallas_call(
        kernel,
        out_shape=(out, out),
        in_specs=[smem, smem, hbm, hbm, hbm, vmem, hbm, vmem, vmem],
        out_specs=(vmem, vmem),
        scratch_shapes=[
            pltpu.VMEM((NX, 2, 8, K, CH), BF16),
            pltpu.VMEM((NX, 2, 8, K, CH), BF16),
            pltpu.VMEM((NX, 4, 8, K, CH), BF16),
            pltpu.VMEM((NX, 4, 8, K, CH), BF16),
            pltpu.VMEM((2, 4, K, CH), BF16),
            pltpu.VMEM((8, 2, 256, 256), BF16),
            pltpu.VMEM((8, 2, 256, 256), BF16),
            pltpu.VMEM((4, 2 * K, 512), BF16),
            pltpu.VMEM((8, 2 * K, 512), BF16),
            pltpu.VMEM((8, K, NB), F32),
            pltpu.VMEM((8, K, NB), F32),
            pltpu.VMEM((8, K, NB), F32),
            pltpu.VMEM((NZ - 1, 2, 16, NB), F32),
            pltpu.VMEM((NZ - 1, 2, 16, NB), F32),
            pltpu.VMEM((NZ - 1, 2, 2, 8, NB), F32),
            pltpu.VMEM((NZ - 1, 2, 2, 8, NB), F32),
            pltpu.VMEM((K, NB), F32),
            pltpu.VMEM((K, NB), BF16),
            pltpu.VMEM((K, NB), BF16),
            pltpu.VMEM((K, 2 * K), F32),
            pltpu.VMEM((K, NB), F32),
            pltpu.VMEM((8, K, K), F32),
            pltpu.VMEM((8, K, 512), F32),
            pltpu.VMEM((32, NB), F32),
            pltpu.VMEM((32, NB), F32),
            pltpu.VMEM((32, NB), F32),
            pltpu.VMEM((32, NB), F32),
            pltpu.SemaphoreType.DMA((N_COPIES,)),
            pltpu.SemaphoreType.DMA((N_COPIES,)),
            pltpu.SemaphoreType.DMA((4,)),
        ],
        compiler_params=pltpu.CompilerParams(
            collective_id=0, has_side_effects=True, vmem_limit_bytes=56 * 1024 * 1024
        ),
        name="trailing_update",
    )(row_mask, col_mask, tile_left, tile_right, row_left, row_right, col_left, col_right, sketch)


def solution(mesh):
    in_specs = (
        P("row", "col", None, None),
        P("row", "col", None, None),
        P("row", "depth", None, "col"),
        P("row", "depth", None, "col"),
        P("col", "depth", None, "row"),
        P("col", "depth", None, "row"),
        P("row", "depth"),
        P("col", "depth"),
        P(),
    )
    out_specs = (P("row", "col", "depth", None), P("row", "col", "depth", None))
    return jax.shard_map(
        on_device, mesh=mesh, in_specs=in_specs, out_specs=out_specs, check_vma=False
    )
```

```python
import math

import jax
import jax.numpy as jnp
from jax import lax
from jax.experimental import pallas as pl
from jax.experimental.pallas import tpu as pltpu
from jax.sharding import PartitionSpec as P

NB = 1024
K = 64
MESH = pl.DeviceIdType.MESH
F32 = jnp.float32
BF16 = jnp.bfloat16
HI = lax.Precision.HIGHEST
NZ = 8
NX = 4
CH = NB // NX


def dot_nn(a, b):
    return lax.dot_general(a, b, (((1,), (0,)), ((), ())), preferred_element_type=F32)


def dot_nt(a, b):
    return lax.dot_general(a, b, (((1,), (1,)), ((), ())), preferred_element_type=F32)


def split2(v):
    hi = v.astype(BF16)
    lo = (v - hi.astype(F32)).astype(BF16)
    return hi, lo


def split3(v):
    hi = v.astype(BF16)
    rest = v - hi.astype(F32)
    mid = rest.astype(BF16)
    lo = (rest - mid.astype(F32)).astype(BF16)
    return hi, mid, lo


def kernel(
    rm, cm, tl_in, tr_in, rl_in, rr_in, cl_in, cr_in, sk,
    outl, outr,
    RR, RL, CR, CL, WV, WS, CSP, BDh, BDl, CS, MX, S, SG, RT, RSP, RSM, RQP, RQM,
    TT, TLO, TRO, X, Q, WP, WW, BC, FSL, FSR, FRL, FRR,
    ssem, rsem, lsem,
):
    d = lax.axis_index("depth")
    x = lax.axis_index("row")
    y = lax.axis_index("col")
    c = lax.rem(d, 2)
    o = 1 - c
    z = lax.div(d, 2)

    def zdev(k):
        return (lax.rem(z + k, NZ) * 2 + c, x, y)

    def xdev(k):
        return (d, lax.rem(x + k, NX), y)

    def ydev(k):
        return (d, x, lax.rem(y + k, NX))

    sib = (z * 2 + o, x, y)

    def chunk(base, k):
        return lax.rem(base + k, NX)

    names = {}
    descs = {}

    def send(name, src, dst, dev):
        n = names.setdefault(name, len(names))
        copy = pltpu.make_async_remote_copy(
            src_ref=src, dst_ref=dst, send_sem=ssem.at[n], recv_sem=rsem.at[n],
            device_id=dev, device_id_type=MESH,
        )
        copy.start()
        descs[name] = copy

    def recv(name):
        descs[name].wait_recv()

    barrier = pltpu.get_barrier_semaphore()
    partners = [zdev(k) for k in range(1, NZ)] + [xdev(1), xdev(3), ydev(1), ydev(3), sib]
    for dev in partners:
        pl.semaphore_signal(barrier, inc=1, device_id=dev, device_id_type=MESH)
    tile_i = 2 * c + lax.div(z, 4)
    tile_j = lax.rem(z, 4)
    local = [
        pltpu.make_async_copy(rr_in.at[pl.ds(2 * c, 2)], RR.at[y, :, pl.ds(4 * c, 4)], lsem.at[0]),
        pltpu.make_async_copy(cr_in, CR.at[x, :, pl.ds(4 * c, 4)], lsem.at[1]),
        pltpu.make_async_copy(rl_in.at[pl.ds(2 * c, 2)], RL.at[y, :, pl.ds(4 * c, 4)], lsem.at[2]),
        pltpu.make_async_copy(cl_in, CL.at[x, :, pl.ds(4 * c, 4)], lsem.at[3]),
        pltpu.make_async_copy(tl_in.at[tile_i, tile_j], TLO, lsem.at[4]),
        pltpu.make_async_copy(tr_in.at[tile_i, tile_j], TRO, lsem.at[5]),
    ]
    for copy in local:
        copy.start()
    pl.semaphore_wait(barrier, len(partners))

    def grp(buf, b, g):
        return buf.at[b, :, pl.ds(4 * g, 4)]

    def half(buf, a, h):
        return buf.at[a, pl.ds(2 * h, 2), pl.ds(4 * c, 4)]

    def part(buf, a, h):
        return buf.at[a, pl.ds(2 * h, 2)]

    def block(buf, b, i, g):
        return buf.at[b, i, pl.ds(4 * (c if g == "c" else o), 4)]

    def rows_own(t, buf, src):
        for i in (0, 1):
            send(f"{t}+{i}c", src.at[2 * c + i], block(buf, y, i, "c"), ydev(1))
            send(f"{t}-{1 - i}c", src.at[2 * c + 1 - i], block(buf, y, 1 - i, "c"), ydev(3))

    def rows_other(t, buf):
        recv(t + "sw")
        for i in (0, 1):
            send(f"{t}+{i}o", block(buf, y, i, "o"), block(buf, y, i, "o"), ydev(1))
            send(f"{t}-{1 - i}o", block(buf, y, 1 - i, "o"), block(buf, y, 1 - i, "o"), ydev(3))

    def rows_on(t, buf, g):
        recv(f"{t}+0{g}")
        send(f"{t}+f{g}", block(buf, chunk(y, 3), 0, g), block(buf, chunk(y, 3), 0, g), ydev(1))
        recv(f"{t}-1{g}")
        send(f"{t}-f{g}", block(buf, chunk(y, 1), 1, g), block(buf, chunk(y, 1), 1, g), ydev(3))

    def rows_end(t):
        for came in ("+1c", "-0c", "+1o", "-0o", "+fc", "-fc", "+fo", "-fo"):
            recv(t + came)

    def cols_own(t, buf, of, src0, src1):
        send(t + "x+0", src0, of(buf, x, 0), xdev(1))
        send(t + "x-1", src1, of(buf, x, 1), xdev(3))
        send(t + "x+1", src1, of(buf, x, 1), xdev(1))
        send(t + "x-0", src0, of(buf, x, 0), xdev(3))

    def cols_on(t, buf, of):
        recv(t + "x+0")
        send(t + "x+f", of(buf, chunk(x, 3), 0), of(buf, chunk(x, 3), 0), xdev(1))
        recv(t + "x-1")
        send(t + "x-f", of(buf, chunk(x, 1), 1), of(buf, chunk(x, 1), 1), xdev(3))

    def cols_to_sib(t, buf, which):
        for came, k, h in which:
            if came in ("x+f", "x-f", "x+1", "x-0"):
                recv(t + came)
            send(t + "s" + came, half(buf, chunk(x, k), h), half(buf, chunk(x, k), h), sib)

    early = (("x+0", 3, 0), ("x-1", 1, 1))
    late = (("x+f", 2, 0), ("x-f", 2, 1), ("x+1", 3, 1), ("x-0", 1, 0))

    def cols_end(t):
        for came in ("", "x+0", "x-1", "x+1", "x-0", "x+f", "x-f"):
            recv(t + "s" + came)

    send("Rsw", rr_in.at[pl.ds(2 * o, 2)], grp(RR, y, c), sib)
    rows_own("R", RR, rr_in)
    cols_own("R", CR, half, cr_in.at[pl.ds(0, 2)], cr_in.at[pl.ds(2, 2)])
    send("Rs", cr_in, CR.at[x, :, pl.ds(4 * c, 4)], sib)
    rows_other("R", RR)
    send("Lsw", rl_in.at[pl.ds(2 * o, 2)], grp(RL, y, c), sib)
    rows_own("L", RL, rl_in)

    of_lane = lax.broadcasted_iota(jnp.int32, (1, 256), 1) // K
    for q in range(8):
        for base, buf in ((2 * c, WV.at[c]), (2 * o, WS)):
            row = jnp.zeros((1, 256), F32)
            for kk in range(4):
                weight = (rm[base + q // 4, kk] * cm[q % 4, kk]).astype(F32)
                row = row + jnp.where(of_lane == kk, weight, 0.0)
            buf[q:q + 1, :] = row
    send("M", WS, WV.at[c], sib)
    for copy in local:
        copy.wait()

    def part_sketch(j, _):
        CSP[x, j] = dot_nt(
            sk[:, pl.ds(pl.multiple_of(CH * x, CH), CH)], CL[x, j, pl.ds(4 * c, 4)].reshape(256, CH)
        )
        return 0

    lax.fori_loop(0, 4, part_sketch, 0)
    cols_own("C", CSP, part, part(CSP, x, 0), part(CSP, x, 1))
    rows_on("R", RR, "c")
    cols_on("R", CR, half)
    rows_on("R", RR, "o")
    rows_other("L", RL)
    cols_to_sib("R", CR, early)

    h, m, l = split3(dot_nt(sk[...], TRO[...]))
    own = dot_nn(jnp.concatenate([h, m, l], axis=0), TLO[...])
    TT[...] = own[0:K] + own[K:2 * K] + own[2 * K:]

    rows_on("L", RL, "c")
    rows_end("R")
    cols_to_sib("R", CR, late)
    cols_on("C", CSP, part)
    cols_end("R")
    recv("M")

    blocks = lax.broadcasted_iota(jnp.int32, (256, 256), 0) // K == lax.broadcasted_iota(jnp.int32, (256, 256), 1) // K

    def couple(n, _):
        q, g = lax.div(n, 2), lax.rem(n, 2)
        i, j = lax.div(q, 4), lax.rem(q, 4)
        acc = jnp.zeros((256, 256), F32)
        for b in range(NX):
            acc = acc + dot_nt(
                RR[b, i, pl.ds(4 * g, 4)].reshape(256, CH), CR[b, j, pl.ds(4 * g, 4)].reshape(256, CH)
            )
        hi, lo = split2(jnp.where(blocks, -acc * WV[g, pl.ds(q, 1), :], 0.0))
        BDh[q, g] = hi
        BDl[q, g] = lo
        return 0

    lax.fori_loop(0, 8, couple, 0)
    rows_on("L", RL, "o")
    lax.fori_loop(8, 16, couple, 0)
    for came in ("x+f", "x-f", "x+1", "x-0"):
        recv("C" + came)

    def col_sketch(j, _):
        hi, lo = split2((CSP[0, j] + CSP[1, j]) + (CSP[2, j] + CSP[3, j]))
        CS[j, c, 0:K] = hi
        CS[j, c, K:2 * K] = lo
        return 0

    lax.fori_loop(0, 4, col_sketch, 0)
    send("CS", CS.at[:, c], CS.at[:, c], sib)
    cols_own("L", CL, half, half(CL, x, 0), half(CL, x, 1))
    send("Ls", CL.at[x, :, pl.ds(4 * c, 4)], CL.at[x, :, pl.ds(4 * c, 4)], sib)
    recv("CS")

    def mix_tile(q, _):
        j = lax.rem(q, 4)
        for g in range(2):
            both = CS[j, g]
            p = dot_nt(both, BDh[q, g])
            mix = p[0:K] + p[K:] + dot_nt(both[0:K], BDl[q, g])
            hi, lo = split2(mix)
            MX[q, 0:K, 256 * g:256 * (g + 1)] = hi
            MX[q, K:2 * K, 256 * g:256 * (g + 1)] = lo
        return 0

    lax.fori_loop(0, 8, mix_tile, 0)
    rows_end("L")

    def s_tile(q):
        i = lax.div(q, 4)
        both = MX[q]
        for b in range(NX):
            p = dot_nn(both, RL[b, i].reshape(512, CH))
            S[q, :, CH * b:CH * (b + 1)] = p[0:K] + p[K:]

    def at(k):
        return lax.rem(z + k, NZ)

    def sum_send(way, s, u):
        buf, dev, tile = (RSP, zdev(1), at(4 - s)) if way == "+" else (RSM, zdev(7), at(4 + s))
        rows = slice(16 * u, 16 * u + 16)
        if s > 1 or (s == 1 and (u < 2) == (way == "+")):
            recv(f"S{way}{s - 1}{u}")
            S[tile, rows] += buf[s - 1, u]
        send(f"S{way}{s}{u}", S.at[tile, pl.ds(16 * u, 16)], buf.at[s, u], dev)

    s_tile(at(4))
    for u in (0, 2, 1, 3):
        sum_send("+" if u < 2 else "-", 0, u)
    s_tile(at(3))
    for u in (2, 3):
        sum_send("+", 1, u)
    s_tile(at(5))
    for u in (0, 1):
        sum_send("-", 1, u)
    s_tile(at(2))
    s_tile(at(6))
    for u in (0, 1):
        sum_send("+", 1, u)
        sum_send("-", 1, u + 2)
    s_tile(at(1))
    s_tile(at(7))
    cols_on("L", CL, half)
    for u in (2, 3, 0, 1):
        sum_send("+", 2, u)
        sum_send("-", 2, (u + 2) % 4)
    s_tile(z)
    cols_to_sib("L", CL, early)
    for u in (2, 3, 0, 1):
        sum_send("+", 3, u)
        sum_send("-", 3, (u + 2) % 4)
    cols_to_sib("L", CL, late)

    def pass_on(s, u, way):
        if s == 4 and (u < 2) != (way == "+"):
            return
        if s > 1:
            recv(f"G{way}{s - 1}{u}")
        part_of = SG.at[at(9 - s) if way == "+" else at(s - 1), pl.ds(16 * u, 16)]
        send(f"G{way}{s}{u}", part_of, part_of, zdev(1 if way == "+" else 7))

    def pass_both(s, n):
        pass_on(s, n, "+")
        pass_on(s, (n + 2) % 4, "-")

    for u in (0, 2, 1, 3):
        recv(f"S+3{u}")
        recv(f"S-3{u}")
        rows = slice(16 * u, 16 * u + 16)
        SG[z, rows] = (S[z, rows] + TT[rows]) + (RSP[3, u] + RSM[3, u])
    for u in range(4):
        pass_both(1, u)

    def tile_back(q):
        i = lax.div(q, 4)
        hi, lo = split2(SG[q])
        both = jnp.concatenate([hi, lo], axis=0)
        acc = jnp.zeros((2 * K, 512), F32)
        for b in range(NX):
            acc = acc + dot_nt(both[:, CH * b:CH * (b + 1)], RL[b, i].reshape(512, CH))
        hi, lo = split2(acc[0:K] + acc[K:])
        both = jnp.concatenate([hi, lo], axis=0)
        for g in range(2):
            cols = slice(256 * g, 256 * (g + 1))
            p = dot_nn(both[:, cols], BDh[q, g])
            BC[q, :, cols] = p[0:K] + p[K:] + dot_nn(hi[:, cols], BDl[q, g])

    lane = lax.broadcasted_iota(jnp.int32, (K, 2 * K), 1)
    sub = lax.broadcasted_iota(jnp.int32, (K, 2 * K), 0)
    lane1 = lax.broadcasted_iota(jnp.int32, (1, 2 * K), 1)
    sub1 = lax.broadcasted_iota(jnp.int32, (K, 1), 0)

    def inverse_factor(v, between=None):
        wide = jnp.concatenate([v, jnp.zeros_like(v)], axis=0)
        gram = lax.dot_general(v, wide, (((1,), (1,)), ((), ())), precision=HI, preferred_element_type=F32)
        X[...] = jnp.where(lane == sub + K, 1.0, gram)

        def step(t, _):
            n = 4 * t
            full = X[...]
            rows = [X[pl.ds(n + e, 1), :] for e in range(4)]
            top = {
                (e, f): jnp.sum(jnp.where(lane1 == n + f, rows[e], 0.0), axis=1, keepdims=True)
                for e in range(4) for f in range(e, 4)
            }
            cols = [jnp.sum(jnp.where(lane == n + e, full, 0.0), axis=1, keepdims=True) for e in range(4)]
            for e in range(4):
                inv = 1.0 / top[e, e]
                for f in range(e + 1, 4):
                    ratio = top[e, f] * inv
                    rows[f] = rows[f] - ratio * rows[e]
                    cols[f] = cols[f] - ratio * cols[e]
                    for w in range(f, 4):
                        top[f, w] = top[f, w] - ratio * top[e, w]
                full = full - jnp.where(sub1 > n + e, cols[e], 0.0) * (rows[e] * inv)
            X[...] = full
            return 0

        lax.fori_loop(0, K // 8, step, 0)
        if between:
            between()
        lax.fori_loop(K // 8, K // 4, step, 0)
        full = X[...]
        pivots = jnp.sum(jnp.where(lane == sub, full, 0.0), axis=1, keepdims=True)
        return full[:, K:] * (1.0 / jnp.sqrt(pivots))

    def dot_hi(a, b):
        return lax.dot_general(a, b, (((1,), (0,)), ((), ())), precision=HI, preferred_element_type=F32)

    first = inverse_factor(SG[z])
    Q[...] = dot_hi(first, SG[z])
    pass_both(2, 0)
    second = inverse_factor(Q[...], lambda: pass_both(2, 1))
    whole = dot_hi(second, first)
    WP[z, :, 0:K] = whole[32:64]
    WP[z, :, K:2 * K] = whole[0:32]
    pass_both(2, 2)
    for k in range(1, NZ):
        send(f"W{k}", WP.at[z], WP.at[z], zdev(k))
    tile_back(z)
    pass_both(2, 3)
    pass_both(3, 0)
    tile_back(at(1))
    pass_both(3, 1)
    tile_back(at(7))
    pass_both(3, 2)
    pass_both(4, 0)
    h, m, l = split3(dot_hi(whole, SG[z]))
    own = dot_nt(jnp.concatenate([h, m, l], axis=0), TLO[...])
    h, m, l = split3(own[0:K] + own[K:2 * K] + own[2 * K:])
    own = dot_nn(jnp.concatenate([h, m, l], axis=0), TRO[...])
    TT[...] = own[0:K] + own[K:2 * K] + own[2 * K:]
    pass_both(3, 3)
    pass_both(4, 1)
    tile_back(at(2))
    tile_back(at(6))
    for u in (2, 3):
        recv(f"G+3{u}")
    tile_back(at(5))
    for u in (0, 1):
        recv(f"G-3{u}")
    tile_back(at(3))
    for u in range(4):
        recv(f"G{'+' if u < 2 else '-'}4{u}")
    tile_back(at(4))
    for k in range(1, NZ):
        recv(f"W{k}")
    cols_end("L")

    def unpack(q, _):
        WW[q, 32:64] = WP[q, :, 0:K]
        WW[q, 0:32] = WP[q, :, K:2 * K]
        return 0

    lax.fori_loop(0, 8, unpack, 0)

    def right_tile(q, _):
        j = lax.rem(q, 4)
        hi, lo = split2(dot_hi(WW[q], BC[q]))
        both = jnp.concatenate([hi, lo], axis=0)
        mine = jnp.where(q == z, 1.0, 0.0)
        for a in range(NX):
            cols = slice(CH * a, CH * (a + 1))
            p = dot_nn(both, CL[a, j].reshape(512, CH))
            RT[q, :, cols] = p[0:K] + p[K:] + mine * TT[:, cols]
        return 0

    def rows_of(chip):
        return pl.ds(pl.multiple_of(8 * chip, 8), 8)

    keep0 = c == 0

    def basis_rows(q):
        v = dot_hi(WW[q, rows_of(z), :], SG[q])
        FSL[4 * q:4 * q + 4] = jnp.where(keep0, v[4:8], v[0:4])
        outl[2 * c + q // 4, q % 4] = jnp.where(keep0, v[0:4], v[4:8])

    def pair(buf, u, chip):
        return buf.at[pl.ds(2 * u, 2), rows_of(chip)]

    for u in range(4):
        lax.fori_loop(2 * u, 2 * u + 2, right_tile, 0)
        if u < 2:
            send(f"P+0{u}", pair(RT, u, at(4)), RQP.at[0, u], zdev(1))
            send(f"P-1{u}", pair(RT, u, at(5)), RQM.at[1, u], zdev(7))
        else:
            send(f"P-0{u}", pair(RT, u, at(4)), RQM.at[0, u], zdev(7))
            send(f"P+1{u}", pair(RT, u, at(3)), RQP.at[1, u], zdev(1))
    basis_rows(0)
    basis_rows(1)
    for s in range(1, 4):
        for u in range(4):
            for way, buf, dev, chip in (("+", RQP, zdev(1), at(4 - s)), ("-", RQM, zdev(7), at(4 + s))):
                if s == 1 and (u < 2) != (way == "+"):
                    continue
                recv(f"P{way}{s - 1}{u}")
                RT[2 * u:2 * u + 2, rows_of(chip)] += buf[s - 1, u]
                send(f"P{way}{s}{u}", pair(RT, u, chip), buf.at[s, u], dev)
        basis_rows(2 * s)
        basis_rows(2 * s + 1)
    send("FL", FSL, FRL, sib)

    for u in range(4):
        recv(f"P+3{u}")
        recv(f"P-3{u}")
        for q in (2 * u, 2 * u + 1):
            v = RT[q, rows_of(z)] + (RQP[3, u, q % 2] + RQM[3, u, q % 2])
            FSR[4 * q:4 * q + 4] = jnp.where(keep0, v[4:8], v[0:4])
            outr[2 * c + q // 4, q % 4] = jnp.where(keep0, v[0:4], v[4:8])
    send("FR", FSR, FRR, sib)
    recv("FL")
    for q in range(8):
        outl[2 * o + q // 4, q % 4] = FRL[4 * q:4 * q + 4]
    recv("FR")
    for q in range(8):
        outr[2 * o + q // 4, q % 4] = FRR[4 * q:4 * q + 4]
    for copy in descs.values():
        copy.wait_send()


N_COPIES = 2 * (13 + 6 + 7) + 6 + 2 + 28 + 28 + 7 + 28 + 2


def on_device(
    tile_left, tile_right, row_left, row_right, col_left, col_right, row_mask, col_mask, sketch
):
    vmem = pl.BlockSpec(memory_space=pltpu.VMEM)
    smem = pl.BlockSpec(memory_space=pltpu.SMEM)
    hbm = pl.BlockSpec(memory_space=pl.ANY)
    out = jax.ShapeDtypeStruct((4, 4, 4, NB), F32)
    basis, projection = pl.pallas_call(
        kernel,
        out_shape=(out, out),
        in_specs=[smem, smem, hbm, hbm, hbm, hbm, hbm, hbm, vmem],
        out_specs=(vmem, vmem),
        scratch_shapes=[
            pltpu.VMEM((NX, 2, 8, K, CH), BF16),
            pltpu.VMEM((NX, 2, 8, K, CH), BF16),
            pltpu.VMEM((NX, 4, 8, K, CH), BF16),
            pltpu.VMEM((NX, 4, 8, K, CH), BF16),
            pltpu.VMEM((2, 8, 256), F32),
            pltpu.VMEM((8, 256), F32),
            pltpu.VMEM((NX, 4, K, 256), F32),
            pltpu.VMEM((8, 2, 256, 256), BF16),
            pltpu.VMEM((8, 2, 256, 256), BF16),
            pltpu.VMEM((4, 2, 2 * K, 256), BF16),
            pltpu.VMEM((8, 2 * K, 512), BF16),
            pltpu.VMEM((8, K, NB), F32),
            pltpu.VMEM((8, K, NB), F32),
            pltpu.VMEM((8, K, NB), F32),
            pltpu.VMEM((4, 4, 16, NB), F32),
            pltpu.VMEM((4, 4, 16, NB), F32),
            pltpu.VMEM((4, 4, 2, 8, NB), F32),
            pltpu.VMEM((4, 4, 2, 8, NB), F32),
            pltpu.VMEM((K, NB), F32),
            pltpu.VMEM((K, NB), BF16),
            pltpu.VMEM((K, NB), BF16),
            pltpu.VMEM((K, 2 * K), F32),
            pltpu.VMEM((K, NB), F32),
            pltpu.VMEM((8, 32, 2 * K), F32),
            pltpu.VMEM((8, K, K), F32),
            pltpu.VMEM((8, K, 512), F32),
            pltpu.VMEM((32, NB), F32),
            pltpu.VMEM((32, NB), F32),
            pltpu.VMEM((32, NB), F32),
            pltpu.VMEM((32, NB), F32),
            pltpu.SemaphoreType.DMA((N_COPIES,)),
            pltpu.SemaphoreType.DMA((N_COPIES,)),
            pltpu.SemaphoreType.DMA((6,)),
        ],
        compiler_params=pltpu.CompilerParams(
            collective_id=0, has_side_effects=True, vmem_limit_bytes=56 * 1024 * 1024
        ),
        name="trailing_update",
    )(row_mask, col_mask, tile_left, tile_right, row_left, row_right, col_left, col_right, sketch)
    return basis * math.sqrt(NB), projection * (1.0 / math.sqrt(NB))


def solution(mesh):
    in_specs = (
        P("row", "col", None, None),
        P("row", "col", None, None),
        P("row", "depth", None, "col"),
        P("row", "depth", None, "col"),
        P("col", "depth", None, "row"),
        P("col", "depth", None, "row"),
        P("row", "depth"),
        P("col", "depth"),
        P(),
    )
    out_specs = (P("row", "col", "depth", None), P("row", "col", "depth", None))
    return jax.shard_map(
        on_device, mesh=mesh, in_specs=in_specs, out_specs=out_specs, check_vma=False
    )
```

```python
import math

import jax
import jax.numpy as jnp
from jax import lax
from jax.experimental import pallas as pl
from jax.experimental.pallas import tpu as pltpu
from jax.sharding import PartitionSpec as P

NB = 1024
K = 64
MESH = pl.DeviceIdType.MESH
F32 = jnp.float32
BF16 = jnp.bfloat16
HI = lax.Precision.HIGHEST
NZ = 8
NX = 4
CH = NB // NX


def dot_nn(a, b):
    return lax.dot_general(a, b, (((1,), (0,)), ((), ())), preferred_element_type=F32)


def dot_nt(a, b):
    return lax.dot_general(a, b, (((1,), (1,)), ((), ())), preferred_element_type=F32)


def split2(v):
    hi = v.astype(BF16)
    lo = (v - hi.astype(F32)).astype(BF16)
    return hi, lo


def split3(v):
    hi = v.astype(BF16)
    rest = v - hi.astype(F32)
    mid = rest.astype(BF16)
    lo = (rest - mid.astype(F32)).astype(BF16)
    return hi, mid, lo


def kernel(
    rm_in, cm_in, tl_in, tr_in, rl_in, rr_in, cl_in, cr_in, sk_in,
    outl, outr,
    RR, RL, CR, CL, WV, WS, CSP, BDh, BDl, CS, MX, S, SG, RT, RSP, RSM, RQP, RQM,
    TT, TLO, TRO, X, Q, WP, WW, BC, FSL, FSR, FRL, FRR,
    sk, rm, cm, ssem, rsem, lsem,
):
    d = lax.axis_index("depth")
    x = lax.axis_index("row")
    y = lax.axis_index("col")
    c = lax.rem(d, 2)
    o = 1 - c
    z = lax.div(d, 2)

    def zdev(k):
        return (lax.rem(z + k, NZ) * 2 + c, x, y)

    def xdev(k):
        return (d, lax.rem(x + k, NX), y)

    def ydev(k):
        return (d, x, lax.rem(y + k, NX))

    sib = (z * 2 + o, x, y)

    def chunk(base, k):
        return lax.rem(base + k, NX)

    names = {}
    descs = {}

    def send(name, src, dst, dev):
        n = names.setdefault(name, len(names))
        copy = pltpu.make_async_remote_copy(
            src_ref=src, dst_ref=dst, send_sem=ssem.at[n], recv_sem=rsem.at[n],
            device_id=dev, device_id_type=MESH,
        )
        copy.start()
        descs[name] = copy

    def recv(name):
        descs[name].wait_recv()

    barrier = pltpu.get_barrier_semaphore()
    partners = [zdev(k) for k in range(1, NZ)] + [xdev(1), xdev(3), ydev(1), ydev(3), sib]
    for dev in partners:
        pl.semaphore_signal(barrier, inc=1, device_id=dev, device_id_type=MESH)
    tile_i = 2 * c + lax.div(z, 4)
    tile_j = lax.rem(z, 4)
    local = [
        pltpu.make_async_copy(rr_in.at[pl.ds(2 * c, 2)], RR.at[y, :, pl.ds(4 * c, 4)], lsem.at[0]),
        pltpu.make_async_copy(cr_in, CR.at[x, :, pl.ds(4 * c, 4)], lsem.at[1]),
        pltpu.make_async_copy(rl_in.at[pl.ds(2 * c, 2)], RL.at[y, :, pl.ds(4 * c, 4)], lsem.at[2]),
        pltpu.make_async_copy(cl_in, CL.at[x, :, pl.ds(4 * c, 4)], lsem.at[3]),
        pltpu.make_async_copy(tl_in.at[tile_i, tile_j], TLO, lsem.at[4]),
        pltpu.make_async_copy(sk_in, sk, lsem.at[6]),
        pltpu.make_async_copy(rm_in, rm, lsem.at[7]),
        pltpu.make_async_copy(cm_in, cm, lsem.at[8]),
        pltpu.make_async_copy(tr_in.at[tile_i, tile_j], TRO, lsem.at[5]),
    ]
    for copy in local:
        copy.start()
    pl.semaphore_wait(barrier, len(partners))

    def grp(buf, b, g):
        return buf.at[b, :, pl.ds(4 * g, 4)]

    def half(buf, a, h):
        return buf.at[a, pl.ds(2 * h, 2), pl.ds(4 * c, 4)]

    def part(buf, a, h):
        return buf.at[a, pl.ds(2 * h, 2)]

    def block(buf, b, i, g):
        return buf.at[b, i, pl.ds(4 * (c if g == "c" else o), 4)]

    def rows_own(t, buf, src):
        for i in (0, 1):
            send(f"{t}+{i}c", src.at[2 * c + i], block(buf, y, i, "c"), ydev(1))
            send(f"{t}-{1 - i}c", src.at[2 * c + 1 - i], block(buf, y, 1 - i, "c"), ydev(3))

    def rows_other(t, buf):
        recv(t + "sw")
        for i in (0, 1):
            send(f"{t}+{i}o", block(buf, y, i, "o"), block(buf, y, i, "o"), ydev(1))
            send(f"{t}-{1 - i}o", block(buf, y, 1 - i, "o"), block(buf, y, 1 - i, "o"), ydev(3))

    def rows_on(t, buf, g):
        recv(f"{t}+0{g}")
        send(f"{t}+f{g}", block(buf, chunk(y, 3), 0, g), block(buf, chunk(y, 3), 0, g), ydev(1))
        recv(f"{t}-1{g}")
        send(f"{t}-f{g}", block(buf, chunk(y, 1), 1, g), block(buf, chunk(y, 1), 1, g), ydev(3))

    def rows_near(t):
        for came in ("+1c", "-0c", "+1o", "-0o"):
            recv(t + came)

    def rows_far(t):
        for came in ("+fc", "-fc", "+fo", "-fo"):
            recv(t + came)

    def cols_own(t, buf, of, src0, src1):
        send(t + "x+0", src0, of(buf, x, 0), xdev(1))
        send(t + "x-1", src1, of(buf, x, 1), xdev(3))
        send(t + "x+1", src1, of(buf, x, 1), xdev(1))
        send(t + "x-0", src0, of(buf, x, 0), xdev(3))

    def cols_on(t, buf, of):
        recv(t + "x+0")
        send(t + "x+f", of(buf, chunk(x, 3), 0), of(buf, chunk(x, 3), 0), xdev(1))
        recv(t + "x-1")
        send(t + "x-f", of(buf, chunk(x, 1), 1), of(buf, chunk(x, 1), 1), xdev(3))

    def cols_to_sib(t, buf, which):
        for came, k, h in which:
            if came in ("x+f", "x-f", "x+1", "x-0"):
                recv(t + came)
            send(t + "s" + came, half(buf, chunk(x, k), h), half(buf, chunk(x, k), h), sib)

    early = (("x+0", 3, 0), ("x-1", 1, 1))
    late = (("x+f", 2, 0), ("x-f", 2, 1), ("x+1", 3, 1), ("x-0", 1, 0))

    def cols_end(t):
        for came in ("", "x+0", "x-1", "x+1", "x-0", "x+f", "x-f"):
            recv(t + "s" + came)

    send("Rsw", rr_in.at[pl.ds(2 * o, 2)], grp(RR, y, c), sib)
    rows_own("R", RR, rr_in)
    cols_own("R", CR, half, cr_in.at[pl.ds(0, 2)], cr_in.at[pl.ds(2, 2)])
    send("Rs", cr_in, CR.at[x, :, pl.ds(4 * c, 4)], sib)
    rows_other("R", RR)
    send("Lsw", rl_in.at[pl.ds(2 * o, 2)], grp(RL, y, c), sib)

    for copy in local:
        copy.wait()

    of_lane = lax.broadcasted_iota(jnp.int32, (1, 256), 1) // K
    for q in range(8):
        for base, buf in ((2 * c, WV.at[c]), (2 * o, WS)):
            row = jnp.zeros((1, 256), F32)
            for kk in range(4):
                weight = (rm[base + q // 4, kk] * cm[q % 4, kk]).astype(F32)
                row = row + jnp.where(of_lane == kk, weight, 0.0)
            buf[q:q + 1, :] = row
    send("M", WS, WV.at[c], sib)
    def part_sketch(j, _):
        CSP[x, j] = dot_nt(
            sk[:, pl.ds(pl.multiple_of(CH * x, CH), CH)], CL[x, j, pl.ds(4 * c, 4)].reshape(256, CH)
        )
        return 0

    lax.fori_loop(0, 4, part_sketch, 0)
    cols_own("C", CSP, part, part(CSP, x, 0), part(CSP, x, 1))
    rows_on("R", RR, "c")
    cols_on("R", CR, half)
    rows_on("R", RR, "o")
    rows_own("L", RL, rl_in)
    rows_other("L", RL)
    cols_to_sib("R", CR, early)

    h, m, l = split3(dot_nt(sk[...], TRO[...]))
    own = dot_nn(jnp.concatenate([h, m, l], axis=0), TLO[...])
    TT[...] = own[0:K] + own[K:2 * K] + own[2 * K:]

    rows_on("L", RL, "c")
    rows_near("R")
    rows_far("R")
    cols_to_sib("R", CR, late)
    cols_on("C", CSP, part)
    cols_end("R")
    recv("M")

    blocks = lax.broadcasted_iota(jnp.int32, (256, 256), 0) // K == lax.broadcasted_iota(jnp.int32, (256, 256), 1) // K

    def couple(n, _):
        q, g = lax.div(n, 2), lax.rem(n, 2)
        i, j = lax.div(q, 4), lax.rem(q, 4)
        acc = jnp.zeros((256, 256), F32)
        for b in range(NX):
            acc = acc + dot_nt(
                RR[b, i, pl.ds(4 * g, 4)].reshape(256, CH), CR[b, j, pl.ds(4 * g, 4)].reshape(256, CH)
            )
        hi, lo = split2(jnp.where(blocks, -acc * WV[g, pl.ds(q, 1), :], 0.0))
        BDh[q, g] = hi
        BDl[q, g] = lo
        return 0

    lax.fori_loop(0, 8, couple, 0)
    rows_on("L", RL, "o")
    lax.fori_loop(8, 16, couple, 0)
    for came in ("x+f", "x-f", "x+1", "x-0"):
        recv("C" + came)

    def col_sketch(j, _):
        hi, lo = split2((CSP[0, j] + CSP[1, j]) + (CSP[2, j] + CSP[3, j]))
        CS[j, c, 0:K] = hi
        CS[j, c, K:2 * K] = lo
        return 0

    lax.fori_loop(0, 4, col_sketch, 0)
    send("CS", CS.at[:, c], CS.at[:, c], sib)
    cols_own("L", CL, half, half(CL, x, 0), half(CL, x, 1))
    send("Ls", CL.at[x, :, pl.ds(4 * c, 4)], CL.at[x, :, pl.ds(4 * c, 4)], sib)
    recv("CS")

    def mix_tile(q):
        j = lax.rem(q, 4)
        for g in range(2):
            both = CS[j, g]
            p = dot_nt(both, BDh[q, g])
            mix = p[0:K] + p[K:] + dot_nt(both[0:K], BDl[q, g])
            hi, lo = split2(mix)
            MX[q, 0:K, 256 * g:256 * (g + 1)] = hi
            MX[q, K:2 * K, 256 * g:256 * (g + 1)] = lo

    rows_near("L")

    parts = (y, chunk(y, 3), chunk(y, 1), chunk(y, 2))

    def s_tile(q, wave):
        if wave[0] == 0:
            mix_tile(q)
        i = lax.div(q, 4)
        both = MX[q]
        for n in range(*wave):
            p = dot_nn(both, RL[parts[n], i].reshape(512, CH))
            S[n, q] = p[0:K] + p[K:]

    def at(k):
        return lax.rem(z + k, NZ)

    def sum_send(wave, way, s, u):
        buf, dev, tile = (RSP, zdev(1), at(4 - s)) if way == "+" else (RSM, zdev(7), at(4 + s))
        ns, nd = slice(*wave), pl.ds(wave[0], wave[1] - wave[0])
        if s > 1 or (s == 1 and (u < 2) == (way == "+")):
            recv(f"S{wave[0]}{way}{s - 1}{u}")
            S[ns, tile, 16 * u:16 * u + 16] += buf[ns, s - 1, u]
        send(f"S{wave[0]}{way}{s}{u}", S.at[nd, tile, pl.ds(16 * u, 16)], buf.at[nd, s, u], dev)

    def sum_start(wave):
        s_tile(at(4), wave)
        for u in (0, 2, 1, 3):
            sum_send(wave, "+" if u < 2 else "-", 0, u)
        s_tile(at(3), wave)
        for u in (2, 3):
            sum_send(wave, "+", 1, u)
        s_tile(at(5), wave)
        for u in (0, 1):
            sum_send(wave, "-", 1, u)

    def sum_one(wave):
        for u in (0, 1):
            sum_send(wave, "+", 1, u)
            sum_send(wave, "-", 1, u + 2)

    def sum_two(wave):
        for u, v in ((2, 0), (0, 2), (3, 1), (1, 3)):
            sum_send(wave, "+", 2, u)
            sum_send(wave, "-", 2, v)

    def sum_three(wave):
        for u in (0, 2, 1, 3):
            sum_send(wave, "+", 3, u)
            sum_send(wave, "-", 3, u)

    near, opposite = (0, 3), (3, 4)
    sum_start(near)
    s_tile(at(2), near)
    s_tile(at(6), near)
    sum_one(near)
    s_tile(at(1), near)
    s_tile(at(7), near)
    rows_far("L")
    sum_start(opposite)
    for k in (2, 6, 1, 7):
        s_tile(at(k), opposite)
    sum_one(opposite)
    sum_two(near)
    cols_on("L", CL, half)
    sum_two(opposite)
    s_tile(z, near)
    s_tile(z, opposite)
    sum_three(near)
    cols_to_sib("L", CL, early)
    sum_three(opposite)
    cols_to_sib("L", CL, late)

    def pass_on(s, u, way):
        if s == 4 and (u < 2) != (way == "+"):
            return
        if s > 1:
            recv(f"G{way}{s - 1}{u}")
        part_of = SG.at[at(9 - s) if way == "+" else at(s - 1), pl.ds(16 * u, 16)]
        send(f"G{way}{s}{u}", part_of, part_of, zdev(1 if way == "+" else 7))

    def pass_both(s, n):
        pass_on(s, (0, 2, 1, 3)[n], "+")
        pass_on(s, (2, 0, 3, 1)[n], "-")

    for u in (0, 2, 1, 3):
        for wave in (near, opposite):
            recv(f"S{wave[0]}+3{u}")
            recv(f"S{wave[0]}-3{u}")
        rows = slice(16 * u, 16 * u + 16)
        for n in range(4):
            cols = pl.ds(pl.multiple_of(CH * parts[n], CH), CH)
            SG[z, rows, cols] = (S[n, z, rows] + TT[rows, cols]) + (RSP[n, 3, u] + RSM[n, 3, u])
        if u >= 2:
            pass_both(1, 2 * (u - 2))
            pass_both(1, 2 * (u - 2) + 1)

    def tile_back(q):
        i = lax.div(q, 4)
        hi, lo = split2(SG[q])
        both = jnp.concatenate([hi, lo], axis=0)
        acc = jnp.zeros((2 * K, 512), F32)
        for b in range(NX):
            acc = acc + dot_nt(both[:, CH * b:CH * (b + 1)], RL[b, i].reshape(512, CH))
        hi, lo = split2(acc[0:K] + acc[K:])
        both = jnp.concatenate([hi, lo], axis=0)
        for g in range(2):
            cols = slice(256 * g, 256 * (g + 1))
            p = dot_nn(both[:, cols], BDh[q, g])
            BC[q, :, cols] = p[0:K] + p[K:] + dot_nn(hi[:, cols], BDl[q, g])

    lane = lax.broadcasted_iota(jnp.int32, (K, 2 * K), 1)
    sub = lax.broadcasted_iota(jnp.int32, (K, 2 * K), 0)
    lane1 = lax.broadcasted_iota(jnp.int32, (1, 2 * K), 1)
    sub1 = lax.broadcasted_iota(jnp.int32, (K, 1), 0)

    def inverse_factor(v, between=None):
        wide = jnp.concatenate([v, jnp.zeros_like(v)], axis=0)
        gram = lax.dot_general(v, wide, (((1,), (1,)), ((), ())), precision=HI, preferred_element_type=F32)
        X[...] = jnp.where(lane == sub + K, 1.0, gram)

        def step(t, _):
            n = 4 * t
            full = X[...]
            rows = [X[pl.ds(n + e, 1), :] for e in range(4)]
            top = {
                (e, f): jnp.sum(jnp.where(lane1 == n + f, rows[e], 0.0), axis=1, keepdims=True)
                for e in range(4) for f in range(e, 4)
            }
            cols = [jnp.sum(jnp.where(lane == n + e, full, 0.0), axis=1, keepdims=True) for e in range(4)]
            for e in range(4):
                inv = 1.0 / top[e, e]
                for f in range(e + 1, 4):
                    ratio = top[e, f] * inv
                    rows[f] = rows[f] - ratio * rows[e]
                    cols[f] = cols[f] - ratio * cols[e]
                    for w in range(f, 4):
                        top[f, w] = top[f, w] - ratio * top[e, w]
                full = full - jnp.where(sub1 > n + e, cols[e], 0.0) * (rows[e] * inv)
            X[...] = full
            return 0

        lax.fori_loop(0, K // 8, step, 0)
        if between:
            between()
        lax.fori_loop(K // 8, K // 4, step, 0)
        full = X[...]
        pivots = jnp.sum(jnp.where(lane == sub, full, 0.0), axis=1, keepdims=True)
        return full[:, K:] * (1.0 / jnp.sqrt(pivots))

    def dot_hi(a, b):
        return lax.dot_general(a, b, (((1,), (0,)), ((), ())), precision=HI, preferred_element_type=F32)

    first = inverse_factor(SG[z])
    Q[...] = dot_hi(first, SG[z])
    pass_both(2, 0)
    second = inverse_factor(Q[...], lambda: pass_both(2, 1))
    whole = dot_hi(second, first)
    WP[z, :, 0:K] = whole[32:64]
    WP[z, :, K:2 * K] = whole[0:32]
    pass_both(2, 2)
    for k in range(1, NZ):
        send(f"W{k}", WP.at[z], WP.at[z], zdev(k))
    tile_back(z)
    pass_both(2, 3)
    pass_both(3, 0)
    tile_back(at(1))
    pass_both(3, 1)
    tile_back(at(7))
    pass_both(3, 2)
    pass_both(4, 0)
    h, m, l = split3(dot_hi(whole, SG[z]))
    own = dot_nt(jnp.concatenate([h, m, l], axis=0), TLO[...])
    h, m, l = split3(own[0:K] + own[K:2 * K] + own[2 * K:])
    own = dot_nn(jnp.concatenate([h, m, l], axis=0), TRO[...])
    TT[...] = own[0:K] + own[K:2 * K] + own[2 * K:]
    pass_both(3, 3)
    pass_both(4, 2)
    tile_back(at(2))
    tile_back(at(6))
    for u in (2, 3):
        recv(f"G+3{u}")
    tile_back(at(5))
    for u in (0, 1):
        recv(f"G-3{u}")
    tile_back(at(3))
    for u in range(4):
        recv(f"G{'+' if u < 2 else '-'}4{u}")
    tile_back(at(4))
    for k in range(1, NZ):
        recv(f"W{k}")
    cols_end("L")

    def unpack(q, _):
        WW[q, 32:64] = WP[q, :, 0:K]
        WW[q, 0:32] = WP[q, :, K:2 * K]
        return 0

    lax.fori_loop(0, 8, unpack, 0)

    def right_tile(q, _):
        j = lax.rem(q, 4)
        hi, lo = split2(dot_hi(WW[q], BC[q]))
        both = jnp.concatenate([hi, lo], axis=0)
        mine = jnp.where(q == z, 1.0, 0.0)
        for a in range(NX):
            cols = slice(CH * a, CH * (a + 1))
            p = dot_nn(both, CL[a, j].reshape(512, CH))
            RT[q, :, cols] = p[0:K] + p[K:] + mine * TT[:, cols]
        return 0

    def rows_of(chip):
        return pl.ds(pl.multiple_of(8 * chip, 8), 8)

    keep0 = c == 0

    def basis_rows(q):
        v = dot_hi(WW[q, rows_of(z), :], SG[q])
        FSL[4 * q:4 * q + 4] = jnp.where(keep0, v[4:8], v[0:4])
        outl[2 * c + q // 4, q % 4] = jnp.where(keep0, v[0:4], v[4:8])

    def pair(buf, u, chip):
        return buf.at[pl.ds(2 * u, 2), rows_of(chip)]

    for u in range(4):
        lax.fori_loop(2 * u, 2 * u + 2, right_tile, 0)
        if u < 2:
            send(f"P+0{u}", pair(RT, u, at(4)), RQP.at[0, u], zdev(1))
            send(f"P-1{u}", pair(RT, u, at(5)), RQM.at[1, u], zdev(7))
        else:
            send(f"P-0{u}", pair(RT, u, at(4)), RQM.at[0, u], zdev(7))
            send(f"P+1{u}", pair(RT, u, at(3)), RQP.at[1, u], zdev(1))
    basis_rows(0)
    basis_rows(1)
    for s in range(1, 4):
        for u in range(4):
            for way, buf, dev, chip in (("+", RQP, zdev(1), at(4 - s)), ("-", RQM, zdev(7), at(4 + s))):
                if s == 1 and (u < 2) != (way == "+"):
                    continue
                recv(f"P{way}{s - 1}{u}")
                RT[2 * u:2 * u + 2, rows_of(chip)] += buf[s - 1, u]
                send(f"P{way}{s}{u}", pair(RT, u, chip), buf.at[s, u], dev)
        basis_rows(2 * s)
        basis_rows(2 * s + 1)
    send("FL", FSL, FRL, sib)

    for u in range(4):
        recv(f"P+3{u}")
        recv(f"P-3{u}")
        for q in (2 * u, 2 * u + 1):
            v = RT[q, rows_of(z)] + (RQP[3, u, q % 2] + RQM[3, u, q % 2])
            FSR[4 * q:4 * q + 4] = jnp.where(keep0, v[4:8], v[0:4])
            outr[2 * c + q // 4, q % 4] = jnp.where(keep0, v[0:4], v[4:8])
        send(f"FR{u}", FSR.at[pl.ds(8 * u, 8)], FRR.at[pl.ds(8 * u, 8)], sib)
    recv("FL")
    for q in range(8):
        outl[2 * o + q // 4, q % 4] = FRL[4 * q:4 * q + 4]
    for u in range(4):
        recv(f"FR{u}")
        for q in (2 * u, 2 * u + 1):
            outr[2 * o + q // 4, q % 4] = FRR[4 * q:4 * q + 4]
    for copy in descs.values():
        copy.wait_send()


N_COPIES = 2 * (13 + 6 + 7) + 6 + 2 + 56 + 28 + 7 + 28 + 5


def on_device(
    tile_left, tile_right, row_left, row_right, col_left, col_right, row_mask, col_mask, sketch
):
    vmem = pl.BlockSpec(memory_space=pltpu.VMEM)
    hbm = pl.BlockSpec(memory_space=pl.ANY)
    out = jax.ShapeDtypeStruct((4, 4, 4, NB), F32)
    basis, projection = pl.pallas_call(
        kernel,
        out_shape=(out, out),
        in_specs=[hbm] * 9,
        out_specs=(vmem, vmem),
        scratch_shapes=[
            pltpu.VMEM((NX, 2, 8, K, CH), BF16),
            pltpu.VMEM((NX, 2, 8, K, CH), BF16),
            pltpu.VMEM((NX, 4, 8, K, CH), BF16),
            pltpu.VMEM((NX, 4, 8, K, CH), BF16),
            pltpu.VMEM((2, 8, 256), F32),
            pltpu.VMEM((8, 256), F32),
            pltpu.VMEM((NX, 4, K, 256), F32),
            pltpu.VMEM((8, 2, 256, 256), BF16),
            pltpu.VMEM((8, 2, 256, 256), BF16),
            pltpu.VMEM((4, 2, 2 * K, 256), BF16),
            pltpu.VMEM((8, 2 * K, 512), BF16),
            pltpu.VMEM((4, 8, K, CH), F32),
            pltpu.VMEM((8, K, NB), F32),
            pltpu.VMEM((8, K, NB), F32),
            pltpu.VMEM((4, 4, 4, 16, CH), F32),
            pltpu.VMEM((4, 4, 4, 16, CH), F32),
            pltpu.VMEM((4, 4, 2, 8, NB), F32),
            pltpu.VMEM((4, 4, 2, 8, NB), F32),
            pltpu.VMEM((K, NB), F32),
            pltpu.VMEM((K, NB), BF16),
            pltpu.VMEM((K, NB), BF16),
            pltpu.VMEM((K, 2 * K), F32),
            pltpu.VMEM((K, NB), F32),
            pltpu.VMEM((8, 32, 2 * K), F32),
            pltpu.VMEM((8, K, K), F32),
            pltpu.VMEM((8, K, 512), F32),
            pltpu.VMEM((32, NB), F32),
            pltpu.VMEM((32, NB), F32),
            pltpu.VMEM((32, NB), F32),
            pltpu.VMEM((32, NB), F32),
            pltpu.VMEM((K, NB), BF16),
            pltpu.SMEM((4, 4), jnp.int32),
            pltpu.SMEM((4, 4), jnp.int32),
            pltpu.SemaphoreType.DMA((N_COPIES,)),
            pltpu.SemaphoreType.DMA((N_COPIES,)),
            pltpu.SemaphoreType.DMA((9,)),
        ],
        compiler_params=pltpu.CompilerParams(
            collective_id=0, has_side_effects=True, vmem_limit_bytes=56 * 1024 * 1024
        ),
        name="trailing_update",
    )(row_mask, col_mask, tile_left, tile_right, row_left, row_right, col_left, col_right, sketch)
    return basis * math.sqrt(NB), projection * (1.0 / math.sqrt(NB))


def solution(mesh):
    in_specs = (
        P("row", "col", None, None),
        P("row", "col", None, None),
        P("row", "depth", None, "col"),
        P("row", "depth", None, "col"),
        P("col", "depth", None, "row"),
        P("col", "depth", None, "row"),
        P("row", "depth"),
        P("col", "depth"),
        P(),
    )
    out_specs = (P("row", "col", "depth", None), P("row", "col", "depth", None))
    return jax.shard_map(
        on_device, mesh=mesh, in_specs=in_specs, out_specs=out_specs, check_vma=False
    )
```
